32 devices in a mesh: hist: 4 (over z), cand: 8 (over y, x, core).
Axes of the slice: x: 2, y: 2, z: 4, core: 2. Of those that a mesh axis runs over, the one named last changes fastest.
Arguments:
- candidates: bfloat16 [8, 256, 1024], P('cand'), may hold values from -6 to 6
- input_gain: float32 [1024], replicated, may hold values from 0.1 to 1.9
- proj_weight: bfloat16 [2, 1024, 1024], P(None, None, 'hist'), may hold values from -0.1875 to 0.1875
- history_cache: bfloat16 [320, 8, 512, 256], P('cand', 'hist'), may hold values from -6 to 6
- slot_user: int32 [320], P('cand'), may hold values from 0 to 7
- slot_block: int32 [320], P('cand'), may hold values from -1 to 31, as said below
- history_len: int32 [8], replicated, may hold values from 1537 to 16384
- attention_gain: float32 [1024], replicated, may hold values from 0.1 to 1.9
- out_weight: bfloat16 [1024, 1024], P(None, 'hist'), may hold values from -0.1875 to 0.1875
Outputs:
- result: bfloat16 [8, 256, 1024], P('cand', None, 'hist')
The draws below stay inside these ranges and needn't reach their ends.
Inputs may be any that keep to these rules, and one draw needn't show every extreme that they name: Each pair of a user u and a block number b < ceil(history_len[u] / 512) is held by exactly one slot; every other slot has slot_block -1.
All inputs are finite; a program needn't handle non-finite values.
Results may differ from the reference program's by a relative error of at most 0.015.
Values may be sent and summed in bfloat16 or wider, within the bound.
No kernel may reach another device: no remote copies, remote signals or barrier semaphores. Data moves between devices by JAX's collectives and lax.ppermute only.
A program may use at most 128 MiB of HBM per device.

```python
import jax
import jax.numpy as jnp
from jax import lax

D = 1024
H = 8
DH = 128
BLK = 512
CANDS = 256
MAXB = 32
USERS = 8
SLOTS = 320


def block_layout(key):
    keys = jax.random.split(key, 5)
    lowest = max(1, MAXB // 8)
    blocks = jax.random.randint(keys[0], (USERS,), lowest, MAXB + 1)
    extra = jax.random.randint(keys[1], (USERS,), 0, BLK)
    lengths = (blocks - 1) * BLK + 1 + extra
    longest = jax.random.randint(keys[2], (), 0, USERS)
    user_ids = jnp.arange(USERS, dtype=jnp.int32)
    lengths = jnp.where(user_ids == longest, MAXB * BLK, lengths)
    blocks = jnp.where(user_ids == longest, MAXB, blocks)
    entry = jnp.arange(SLOTS, dtype=jnp.int32)
    entry_user = jnp.minimum(entry // MAXB, USERS - 1)
    entry_block = entry % MAXB
    filler_user = jax.random.randint(keys[3], (SLOTS,), 0, USERS)
    in_table = entry < USERS * MAXB
    owner_blocks = jnp.sum(jnp.where(entry_user[:, None] == user_ids[None, :], blocks[None, :], 0), axis=1)
    is_live = in_table & (entry_block < owner_blocks)
    user_of_entry = jnp.where(in_table, entry_user, filler_user)
    block_of_entry = jnp.where(is_live, entry_block, -1)
    order = jax.random.permutation(keys[4], SLOTS)
    slot_users = jnp.zeros((SLOTS,), jnp.int32).at[order].set(user_of_entry.astype(jnp.int32))
    slot_blocks = jnp.zeros((SLOTS,), jnp.int32).at[order].set(block_of_entry.astype(jnp.int32))
    return (lengths.astype(jnp.int32), slot_users, slot_blocks)


def draw_slot_user(key, part):
    lengths, slot_users, slot_blocks = block_layout(key)
    return slot_users


def draw_slot_block(key, part):
    lengths, slot_users, slot_blocks = block_layout(key)
    return slot_blocks


def draw_history_len(key, part):
    lengths, slot_users, slot_blocks = block_layout(key)
    return lengths


def steps_of(stream_key, shape, cuts, least, high):
    def one(dim, blocks):
        steps = jax.random.uniform(jax.random.fold_in(jax.random.fold_in(stream_key, 6), dim), (blocks,), jnp.float32, least / len(cuts), high / len(cuts))
        return jnp.repeat(jnp.exp(steps), shape[dim] // blocks).reshape((-1,) + (1,) * (len(shape) - dim - 1))

    level = one(*cuts[0])
    for cut in cuts[1:]:
        level = level * one(*cut)
    return level


def scatter_about(rng, extent, spread, reach, shards=(), kind=jnp.bfloat16):
    loudness = steps_of(rng, extent, shards, -0.22, 0.18) if shards else 1.0
    entries = jax.random.normal(rng, extent, jnp.float32) * spread * loudness
    return jnp.minimum(jnp.maximum(entries, -reach), reach).astype(kind)


def setup_inputs(seed: int = 0) -> dict:
    key_of = jax.random.split(jax.random.key(seed), 10)
    candidates = scatter_about(key_of[0], (USERS, CANDS, D), 1.0, 6.0, ((0, 8),))
    input_gain = jnp.clip(1.0 + 0.18 * jax.random.normal(key_of[1], (D,), jnp.float32), 0.1, 1.9)
    proj_weight = scatter_about(key_of[2], (2, D, D), D ** -0.5, 0.1875, ((2, 4),))
    history_cache = scatter_about(key_of[3], (SLOTS, H, BLK, 2 * DH), 1.0, 6.0, ((0, 8), (1, 4)))
    slot_user = draw_slot_user(jax.random.fold_in(key_of[9], 71), 0)
    slot_block = draw_slot_block(jax.random.fold_in(key_of[9], 71), 0)
    history_len = draw_history_len(jax.random.fold_in(key_of[9], 71), 0)
    attention_gain = jnp.clip(1.0 + 0.18 * jax.random.normal(key_of[7], (D,), jnp.float32), 0.1, 1.9)
    out_weight = scatter_about(key_of[8], (D, D), D ** -0.5, 0.1875, ((1, 4),))
    return {"candidates": candidates, "input_gain": input_gain, "proj_weight": proj_weight, "history_cache": history_cache, "slot_user": slot_user, "slot_block": slot_block, "history_len": history_len, "attention_gain": attention_gain, "out_weight": out_weight}


def layer_norm(rows, gain):
    row_mean = lax.optimization_barrier(jnp.mean(rows, axis=-1, keepdims=True))
    centred = rows - row_mean
    row_var = lax.optimization_barrier(jnp.mean(centred * centred, axis=-1, keepdims=True))
    return centred * lax.rsqrt(row_var + 1e-05) * gain

def reference(candidates, input_gain, proj_weight, history_cache, slot_user, slot_block, history_len, attention_gain, out_weight):
    cand_rows = candidates.astype(jnp.float32)
    normed_input = layer_norm(cand_rows, input_gain.astype(jnp.float32)).astype(jnp.bfloat16)
    flat_rows = normed_input.reshape(USERS * CANDS, D)
    gate_all = jax.nn.silu(jnp.dot(flat_rows, proj_weight[0], preferred_element_type=jnp.float32)).astype(jnp.bfloat16).reshape(USERS, CANDS, D)
    query_all = jax.nn.silu(jnp.dot(flat_rows, proj_weight[1], preferred_element_type=jnp.float32)).astype(jnp.bfloat16).reshape(USERS, CANDS, D)
    event_index = jnp.arange(BLK, dtype=jnp.int32)
    score_scale = DH ** (-0.5)

    def add_slot(carry, items):
        cache_block, owner, position = items
        query = lax.dynamic_index_in_dim(query_all, owner, 0, keepdims=False).astype(jnp.float32).reshape(CANDS, H, DH)
        cache_keys = cache_block[..., :DH].astype(jnp.float32)
        cache_values = cache_block[..., DH:].astype(jnp.float32)
        scores = jnp.einsum('chd,htd->hct', query, cache_keys) * score_scale
        length = lax.dynamic_index_in_dim(history_len, owner, 0, keepdims=False)
        live_mask = (position >= 0) & (position * BLK + event_index < length)
        weights = (jax.nn.silu(scores) * live_mask.astype(jnp.float32)).astype(jnp.bfloat16)
        weights = lax.optimization_barrier(weights).astype(jnp.float32)
        contrib = jnp.einsum('hct,htd->chd', weights, cache_values).reshape(CANDS, D)
        current = lax.dynamic_index_in_dim(carry, owner, 0, keepdims=False)
        carry = lax.dynamic_update_index_in_dim(carry, current + contrib, owner, 0)
        return (carry, None)
    attention, _ = lax.scan(add_slot, jnp.zeros((USERS, CANDS, D), jnp.float32), (history_cache, slot_user, slot_block))
    gated = (layer_norm(attention, attention_gain.astype(jnp.float32)) * gate_all.astype(jnp.float32)).astype(jnp.bfloat16)
    result = cand_rows + jnp.dot(gated.reshape(USERS * CANDS, D), out_weight, preferred_element_type=jnp.float32).reshape(USERS, CANDS, D)
    return result.astype(jnp.bfloat16)
```

```python
import functools

import jax
import jax.numpy as jnp
from jax import lax
from jax.experimental import pallas as pl
from jax.experimental.pallas import tpu as pltpu
from jax.sharding import PartitionSpec as P

D = 1024
DH = 128
EPS = 1e-05
UNIT = 2
BUFS = 6
F32 = jnp.float32
BF16 = jnp.bfloat16
VMEM_BYTES = 32 * 1024 * 1024
HALF_SCALE = 0.5 * DH ** (-0.5)

VM = pl.BlockSpec(memory_space=pltpu.VMEM)
SM = pl.BlockSpec(memory_space=pltpu.SMEM)
HB = pl.BlockSpec(memory_space=pltpu.HBM)
ANY = pl.BlockSpec(memory_space=pl.ANY)


def params():
    return pltpu.CompilerParams(vmem_limit_bytes=VMEM_BYTES)


def silu_of_half(half):
    return half * jnp.tanh(half) + half


SLOT, OFFSET, LIVE, COUNT = range(4)


def project_kernel(
    block_len, cand_hbm, gain_hbm, weight_hbm, user_hbm, block_hbm, len_hbm, *refs
):
    heads = len(refs) - 10
    queries, gate_ref, plan = refs[:heads], refs[heads], refs[heads + 1]
    cand, gain, weight, user, block, length, sems = refs[heads + 2 : heads + 9]
    wsems = refs[heads + 9]
    ints = [
        pltpu.make_async_copy(src, dst, sems.at[i])
        for i, (src, dst) in enumerate([(user_hbm, user), (block_hbm, block), (len_hbm, length)])
    ]
    rows_in = [
        pltpu.make_async_copy(src, dst, sems.at[3 + i])
        for i, (src, dst) in enumerate([(cand_hbm, cand), (gain_hbm, gain)])
    ]
    weights_in = [
        pltpu.make_async_copy(weight_hbm.at[i], weight.at[i], wsems.at[i]) for i in range(2)
    ]
    for copy in ints + rows_in + weights_in[::-1]:
        copy.start()
    me = lax.axis_index("cand")
    slots = user.shape[0]
    for copy in ints:
        copy.wait()

    def note(parity, s, count):
        owner = user[s]
        number = block[s]
        offset = owner ^ me
        plan[SLOT, count] = s
        plan[OFFSET, count] = offset
        plan[LIVE, count] = length[owner] - number * block_len
        return count + ((number >= 0) & (offset % 2 == parity)).astype(jnp.int32)

    odd = lax.fori_loop(0, slots, functools.partial(note, 1), jnp.int32(0))
    count = lax.fori_loop(0, slots, functools.partial(note, 0), odd)
    for i in range(UNIT):
        plan[SLOT, count + i] = 0
        plan[OFFSET, count + i] = 0
        plan[LIVE, count + i] = 0
    plan[COUNT, 0] = odd
    plan[COUNT, 1] = count

    for copy in rows_in:
        copy.wait()
    rows = cand[0].astype(F32)
    centred = rows - jnp.mean(rows, axis=-1, keepdims=True)
    var = jnp.mean(centred * centred, axis=-1, keepdims=True)
    normed = (centred * lax.rsqrt(var + EPS) * gain[...]).astype(BF16)
    weights_in[1].wait()
    half = 0.5 * jnp.dot(normed, weight[1], preferred_element_type=F32)
    query = (silu_of_half(half) * HALF_SCALE).astype(BF16)
    for j in range(heads):
        queries[j][...] = query[:, j * DH : (j + 1) * DH]
    weights_in[0].wait()
    half = 0.5 * jnp.dot(normed, weight[0], preferred_element_type=F32)
    gate_ref[...] = silu_of_half(half).astype(BF16)


def project(candidates, input_gain, proj_weight, slot_user, slot_block, history_len, block_len):
    rows, cols = candidates.shape[1], proj_weight.shape[2]
    slots = slot_user.shape[0]
    heads = cols // DH
    width = -(-(slots + UNIT) // 128) * 128
    outs = pl.pallas_call(
        functools.partial(project_kernel, block_len),
        out_shape=[jax.ShapeDtypeStruct((rows, DH), BF16)] * heads
        + [jax.ShapeDtypeStruct((rows, cols), BF16), jax.ShapeDtypeStruct((4, width), jnp.int32)],
        in_specs=[HB] * 6,
        out_specs=[VM] * (heads + 1) + [SM],
        scratch_shapes=[
            pltpu.VMEM(candidates.shape, BF16),
            pltpu.VMEM((1, D), F32),
            pltpu.VMEM(proj_weight.shape, BF16),
            pltpu.SMEM(slot_user.shape, jnp.int32),
            pltpu.SMEM(slot_block.shape, jnp.int32),
            pltpu.SMEM(history_len.shape, jnp.int32),
            pltpu.SemaphoreType.DMA((5,)),
            pltpu.SemaphoreType.DMA((2,)),
        ],
        compiler_params=params(),
        cost_estimate=pl.CostEstimate(
            flops=4 * rows * cols * D, bytes_accessed=6 * cols * D, transcendentals=2 * rows * cols
        ),
        name="project",
    )(candidates, input_gain, proj_weight, slot_user, slot_block, history_len)
    return outs[:heads], outs[heads], outs[heads + 1]


def attend_kernel(head, which, users, afters, plan, *refs):
    queries, cache, outs = refs[:users], refs[users], refs[users + afters + 1 : -5]
    held, total, kv, wts, sems = refs[-5:]
    block_len = cache.shape[2]
    half = block_len // 2
    start = plan[COUNT, 0] if which == "even" else 0
    stop = plan[COUNT, 0] if which == "odd" else plan[COUNT, 1]
    steps = (stop - start + UNIT - 1) // UNIT

    def fetch(u, g):
        buf = lax.rem(u, BUFS)
        slot = plan[SLOT, start + u * UNIT + g]
        return pltpu.make_async_copy(cache.at[slot, head], kv.at[buf, g], sems.at[buf, g])

    def place(u, g):
        off = plan[OFFSET, start + u * UNIT + g]
        return off if which == "all" else off // 2

    for u in range(BUFS):

        @pl.when(u < steps)
        def _():
            for g in range(UNIT):
                fetch(jnp.int32(u), g).start()

    for d in range(users):
        held[d] = queries[d][...]
    total[...] = jnp.zeros_like(total)

    def arrive(u):
        buf = lax.rem(u, BUFS)
        for g in range(UNIT):
            fetch(u, g).wait()
            at = start + u * UNIT + g
            live = jnp.where(at < stop, plan[LIVE, at], 0)

            @pl.when(live < block_len)
            def _():
                event = lax.broadcasted_iota(jnp.int32, (block_len, DH), 0)
                vals = kv[buf, g, :, DH:]
                kv[buf, g, :, DH:] = jnp.where(event < live, vals, jnp.zeros_like(vals))

    def weigh(u, g, e):
        buf = lax.rem(u, BUFS)
        scores = lax.dot_general(
            held[place(u, g)],
            kv[buf, g, e * half : (e + 1) * half, :DH],
            (((1,), (1,)), ((), ())),
            preferred_element_type=F32,
        )
        wts[g, e] = silu_of_half(scores).astype(BF16)

    def value(u, g, e):
        buf = lax.rem(u, BUFS)
        return jnp.dot(
            wts[g, e], kv[buf, g, e * half : (e + 1) * half, DH:], preferred_element_type=F32
        )

    def gather(u, then):
        for g in range(UNIT):
            acc = value(u, g, 0)
            then(g, 0)
            acc = acc + value(u, g, 1)
            then(g, 1)
            total[place(u, g)] += acc

    @pl.when(steps > 0)
    def _():
        arrive(jnp.int32(0))
        for g in range(UNIT):
            for e in range(2):
                weigh(jnp.int32(0), g, e)

        def step(u, carry):
            arrive(u)
            gather(u - 1, lambda g, e: weigh(u, g, e))

            @pl.when(u - 1 + BUFS < steps)
            def _():
                for g in range(UNIT):
                    fetch(u - 1 + BUFS, g).start()

            return carry

        lax.fori_loop(1, steps, step, 0)
        gather(steps - 1, lambda g, e: None)

    if which == "all":
        near, far = outs
        for d in range(users):
            if d % 2 == 0:
                near[d // 2] = total[d]
            else:
                far[d // 2] = total[d].astype(BF16)
    else:
        outs[0][...] = total[...].astype(outs[0].dtype)


def attend(queries, history_cache, plan, head, which, after):
    users = len(queries)
    rows = queries[0].shape[0]
    slots, _, block_len, width = history_cache.shape
    near = jax.ShapeDtypeStruct((users // (2 if which == "all" else 1), rows, DH), F32)
    far = jax.ShapeDtypeStruct(near.shape, BF16)
    outs = {"all": [near, far], "even": [near], "odd": [far]}[which]
    share = 1 if which == "all" else 2
    return pl.pallas_call(
        functools.partial(attend_kernel, head, which, users, len(after)),
        out_shape=outs,
        in_specs=[SM] + [VM] * users + [HB] + [ANY] * len(after),
        out_specs=[VM] * len(outs),
        scratch_shapes=[
            pltpu.VMEM((users, rows, DH), BF16),
            pltpu.VMEM((users, rows, DH), F32),
            pltpu.VMEM((BUFS, UNIT, block_len, width), BF16),
            pltpu.VMEM((UNIT, 2, rows, block_len // 2), BF16),
            pltpu.SemaphoreType.DMA((BUFS, UNIT)),
        ],
        compiler_params=params(),
        cost_estimate=pl.CostEstimate(
            flops=2 * slots * rows * block_len * width // share,
            bytes_accessed=2 * slots * block_len * width // share,
            transcendentals=slots * rows * block_len // share,
        ),
        name=f"attend_{head}_{which}",
    )(plan, *queries, history_cache, *after)


def pair_kernel(chips, near, far, *refs):
    own, *sends = refs[-chips:]
    own[...] = near[0] + far[0].astype(F32)
    for e, send in enumerate(sends, 1):
        send[...] = (near[e] + far[e].astype(F32)).astype(BF16)


def pair_terms(near, far, after):
    chips, rows, cols = near.shape
    outs = [jax.ShapeDtypeStruct((rows, cols), F32)]
    outs += [jax.ShapeDtypeStruct((rows, cols), BF16)] * (chips - 1)
    return pl.pallas_call(
        functools.partial(pair_kernel, chips),
        out_shape=outs,
        in_specs=[VM] * 2 + [ANY] * len(after),
        out_specs=[VM] * chips,
        compiler_params=params(),
        name="pair_terms",
    )(near, far, *after)


def add_kernel(*refs):
    acc = refs[0][...]
    for ref in refs[1:-1]:
        acc = acc + ref[...].astype(F32)
    refs[-1][...] = acc.astype(BF16)


def add_terms(terms):
    return pl.pallas_call(
        add_kernel,
        out_shape=jax.ShapeDtypeStruct(terms[0].shape, BF16),
        in_specs=[VM] * len(terms),
        out_specs=VM,
        compiler_params=params(),
        name="add_terms",
    )(*terms)


def finish_kernel(shape, cand_ref, gain_ref, weight_ref, *refs):
    parts = len(shape)
    out_ref, refs = refs[-1], list(refs[:-1])
    gate = [refs.pop(0) for _ in range(parts)]
    blocks = [
        jnp.concatenate(
            [sum(refs.pop(0)[...].astype(F32) for _ in range(n)) for n in counts], axis=-1
        )
        for counts in shape
    ]
    me = lax.axis_index("hist")
    cols = out_ref.shape[2]
    mean = sum(jnp.sum(b, axis=-1, keepdims=True) for b in blocks) / D
    blocks = [b - mean for b in blocks]
    var = sum(jnp.sum(b * b, axis=-1, keepdims=True) for b in blocks) / D
    rstd = lax.rsqrt(var + EPS)
    acc = cand_ref[0, :, pl.ds(pl.multiple_of(me * cols, DH), cols)].astype(F32)
    for k in range(parts):
        at = pl.ds(pl.multiple_of((me ^ k) * cols, DH), cols)
        gained = blocks[k] * rstd * gain_ref[:, at]
        gated = (gained * gate[k][...].astype(F32)).astype(BF16)
        acc = acc + jnp.dot(gated, weight_ref[at, :], preferred_element_type=F32)
    out_ref[0] = acc.astype(BF16)


def finish(candidates, attention_gain, out_weight, gate, attn):
    rows, cols = gate[0].shape
    shape = [[len(group) for group in heads] for heads in attn]
    flat = [x for heads in attn for group in heads for x in group]
    return pl.pallas_call(
        functools.partial(finish_kernel, shape),
        out_shape=jax.ShapeDtypeStruct((1, rows, cols), BF16),
        in_specs=[VM] * (3 + len(gate) + len(flat)),
        out_specs=VM,
        compiler_params=params(),
        name="finish",
    )(candidates, attention_gain.reshape(1, D), out_weight, *gate, *flat)


def swap(x, axis, bit):
    n = lax.axis_size(axis)
    return lax.ppermute(x, axis, [(i, i ^ bit) for i in range(n)])


def exchange(x, axis):
    n = lax.axis_size(axis)
    if n != 4:
        return [[x]] + [[swap(x, axis, k)] for k in range(1, n)]
    one, two = swap(x, axis, 1), swap(x, axis, 2)
    mid = lax.ppermute(x, axis, [(1, 2), (2, 1)])
    ends = lax.ppermute(two, axis, [(2, 3), (1, 0)])
    return [[x], [one], [two], [mid, ends]]


def spread(x, users):
    near = [x] + [swap(x, "cand", d) for d in range(2, users, 2)]
    out = []
    for y in near:
        out += [y, swap(y, "cand", 1)]
    return out


def local(
    candidates,
    input_gain,
    proj_weight,
    history_cache,
    slot_user,
    slot_block,
    history_len,
    attention_gain,
    out_weight,
):
    users = lax.axis_size("cand")
    parts = lax.axis_size("hist")
    in_hbm = functools.partial(pltpu.with_memory_space_constraint, memory_space=pltpu.HBM)
    history_cache = in_hbm(history_cache)
    query_own, gate_own, plan = project(
        in_hbm(candidates),
        in_hbm(input_gain.reshape(1, D)),
        in_hbm(proj_weight),
        in_hbm(slot_user),
        in_hbm(slot_block),
        in_hbm(history_len),
        history_cache.shape[2],
    )
    heads = len(query_own)
    queries = [spread(q, users) for q in query_own]
    gate = [gate_own] + [swap(gate_own, "hist", k) for k in range(1, parts)]
    sums, after = [], []
    for j in range(heads):
        if j < heads - 1:
            near, far = attend(queries[j], history_cache, plan, j, "all", after)
        else:
            (far,) = attend(queries[j][1::2], history_cache, plan, j, "odd", after + gate[1:])
            after = [far] + [terms[0] for terms in sums[-1:]]
            (near,) = attend(queries[j][0::2], history_cache, plan, j, "even", after)
        after = [near]
        sums = [add_terms(terms) if isinstance(terms, list) else terms for terms in sums]
        terms = pair_terms(near, swap(far, "cand", 1), sums)
        sums.append([terms[0]] + [swap(t, "cand", 2 * e) for e, t in enumerate(terms[1:], 1)])
    sums[-1] = add_terms(sums[-1])
    attn = [exchange(x, "hist") for x in sums]
    attn = [[attn[j][k] for j in range(heads)] for k in range(parts)]
    return finish(candidates, attention_gain, out_weight, gate, attn)


def solution(mesh):
    return jax.shard_map(
        local,
        mesh=mesh,
        in_specs=(
            P("cand", None, None),
            P(),
            P(None, None, "hist"),
            P("cand", "hist", None, None),
            P("cand"),
            P("cand"),
            P(),
            P(),
            P(None, "hist"),
        ),
        out_specs=P("cand", None, "hist"),
        check_vma=False,
    )
```

```python
import functools

import jax
import jax.numpy as jnp
from jax import lax
from jax.experimental import pallas as pl
from jax.experimental.pallas import tpu as pltpu
from jax.sharding import PartitionSpec as P

D = 1024
DH = 128
EPS = 1e-05
GROUPS = 4
F32 = jnp.float32
BF16 = jnp.bfloat16
VMEM_BYTES = 12 * 1024 * 1024
CACHE_BYTES = 26 * 1024 * 1024
HALF_SCALE = 0.5 * DH ** (-0.5)

VM = pl.BlockSpec(memory_space=pltpu.VMEM)
SM = pl.BlockSpec(memory_space=pltpu.SMEM)
HB = pl.BlockSpec(memory_space=pltpu.HBM)
ANY = pl.BlockSpec(memory_space=pl.ANY)


def params(limit=VMEM_BYTES):
    return pltpu.CompilerParams(vmem_limit_bytes=limit)


def silu_of_half(half):
    return half * jnp.tanh(half) + half


SLOT, OFFSET, LIVE, COUNT = range(4)


def groups_of(chips):
    per = -(-(chips - 1) // (GROUPS - 1))
    return [[0]] + [list(range(at, min(at + per, chips))) for at in range(1, chips, per)]


def project_kernel(
    block_len, per, cand_hbm, gain_hbm, weight_hbm, user_hbm, block_hbm, len_hbm, *refs
):
    query_ref, gate_ref, plan, cand, gain, weight, user, block, length, sems, wsems = refs
    ints = [
        pltpu.make_async_copy(src, dst, sems.at[i])
        for i, (src, dst) in enumerate([(user_hbm, user), (block_hbm, block), (len_hbm, length)])
    ]
    rows_in = [
        pltpu.make_async_copy(src, dst, sems.at[3 + i])
        for i, (src, dst) in enumerate([(cand_hbm, cand), (gain_hbm, gain)])
    ]
    weights_in = [
        pltpu.make_async_copy(weight_hbm.at[i], weight.at[i], wsems.at[i]) for i in range(2)
    ]
    for copy in ints + rows_in + weights_in[::-1]:
        copy.start()
    me = lax.axis_index("cand")
    for copy in ints:
        copy.wait()
    for group in range(GROUPS):
        plan[group, COUNT, 0] = 0
    for s in range(user.shape[0]):
        owner, number = user[s], block[s]
        offset = owner ^ me
        group = (offset // 2 + per - 1) // per
        count = plan[group, COUNT, 0]
        live = jnp.where(number >= 0, length[owner] - number * block_len, 0)
        plan[group, SLOT, count] = s
        plan[group, OFFSET, count] = offset - jnp.where(group > 0, 2 * ((group - 1) * per + 1), 0)
        plan[GROUPS, LIVE, s] = live
        plan[group, COUNT, 0] = count + (number >= 0).astype(jnp.int32)

    for copy in rows_in:
        copy.wait()
    rows = cand[0].astype(F32)
    centred = rows - jnp.mean(rows, axis=-1, keepdims=True)
    var = jnp.mean(centred * centred, axis=-1, keepdims=True)
    normed = (centred * lax.rsqrt(var + EPS) * gain[...]).astype(BF16)
    weights_in[1].wait()
    half = 0.5 * jnp.dot(normed, weight[1], preferred_element_type=F32)
    query_ref[...] = (silu_of_half(half) * HALF_SCALE).astype(BF16)
    weights_in[0].wait()
    half = 0.5 * jnp.dot(normed, weight[0], preferred_element_type=F32)
    gate_ref[...] = silu_of_half(half).astype(BF16)


def project(
    candidates, input_gain, proj_weight, slot_user, slot_block, history_len, block_len, chips
):
    rows, cols = candidates.shape[1], proj_weight.shape[2]
    width = -(-(slot_user.shape[0] + 1) // 128) * 128
    per = -(-(chips - 1) // (GROUPS - 1))
    return pl.pallas_call(
        functools.partial(project_kernel, block_len, per),
        out_shape=[
            jax.ShapeDtypeStruct((rows, cols), BF16),
            jax.ShapeDtypeStruct((rows, cols), BF16),
            jax.ShapeDtypeStruct((GROUPS + 1, 4, width), jnp.int32),
        ],
        in_specs=[HB] * 6,
        out_specs=[VM, VM, SM],
        scratch_shapes=[
            pltpu.VMEM(candidates.shape, BF16),
            pltpu.VMEM((1, D), F32),
            pltpu.VMEM(proj_weight.shape, BF16),
            pltpu.SMEM(slot_user.shape, jnp.int32),
            pltpu.SMEM(slot_block.shape, jnp.int32),
            pltpu.SMEM(history_len.shape, jnp.int32),
            pltpu.SemaphoreType.DMA((5,)),
            pltpu.SemaphoreType.DMA((2,)),
        ],
        compiler_params=params(),
        cost_estimate=pl.CostEstimate(
            flops=4 * rows * cols * D, bytes_accessed=6 * cols * D, transcendentals=2 * rows * cols
        ),
        name="project",
    )(candidates, input_gain, proj_weight, slot_user, slot_block, history_len)


def load_kernel(plan, cache, kv, sems):
    slots, heads, block_len, _ = cache.shape

    def each_live(do):
        def visit(s, carry):
            @pl.when(plan[GROUPS, LIVE, s] > 0)
            def _():
                do(s)

            return carry

        lax.fori_loop(0, slots, visit, 0)

    def copy(s):
        return pltpu.make_async_copy(cache.at[s], kv.at[s], sems.at[s])

    def arrive(s):
        copy(s).wait()
        live = plan[GROUPS, LIVE, s]

        @pl.when(live < block_len)
        def _():
            event = lax.broadcasted_iota(jnp.int32, (block_len, DH), 0)
            for j in range(heads):
                vals = kv[s, j, :, DH:]
                kv[s, j, :, DH:] = jnp.where(event < live, vals, jnp.zeros_like(vals))

    each_live(lambda s: copy(s).start())
    each_live(arrive)


def load(plan, history_cache):
    return pl.pallas_call(
        load_kernel,
        out_shape=pltpu.VMEM(history_cache.shape, BF16),
        in_specs=[SM, HB],
        out_specs=VM,
        scratch_shapes=[pltpu.SemaphoreType.DMA((history_cache.shape[0],))],
        compiler_params=params(CACHE_BYTES),
        cost_estimate=pl.CostEstimate(
            flops=0, bytes_accessed=2 * history_cache.size, transcendentals=0
        ),
        name="load",
    )(plan, history_cache)


def attend_kernel(group, offsets, afters, plan, kv, *refs):
    queries, (near, far, query, total, wts) = refs[:offsets], refs[offsets + afters :]
    heads, block_len = kv.shape[1:3]
    half = block_len // 2
    tiles = [(j, e) for j in range(heads) for e in range(2)]
    count = plan[group, COUNT, 0]

    for d in range(offsets):
        query[d] = queries[d][...]
    total[...] = jnp.zeros_like(total)
    wts[...] = jnp.zeros_like(wts)

    def weigh(u, t):
        j, e = tiles[t]
        scores = lax.dot_general(
            query[plan[group, OFFSET, u], :, j * DH : (j + 1) * DH],
            kv[plan[group, SLOT, u], j, e * half : (e + 1) * half, :DH],
            (((1,), (1,)), ((), ())),
            preferred_element_type=F32,
        )
        wts[t] = silu_of_half(scores).astype(BF16)

    def gather(u, t):
        j, e = tiles[t]
        total[plan[group, OFFSET, u], :, j * DH : (j + 1) * DH] += jnp.dot(
            wts[t],
            kv[plan[group, SLOT, u], j, e * half : (e + 1) * half, DH:],
            preferred_element_type=F32,
        )

    last = len(tiles) - 1

    def step(u, carry):
        for t in range(len(tiles)):
            weigh(u, t)
            if t == 0:
                gather(jnp.maximum(u - 1, 0), last)
            else:
                gather(u, t - 1)
        return carry

    @pl.when(count > 0)
    def _():
        lax.fori_loop(0, count, step, 0)
        gather(count - 1, last)

    for d in range(offsets):
        if d % 2 == 0:
            near[d // 2] = total[d]
        else:
            far[d // 2] = total[d].astype(BF16)


def attend(queries, kv, plan, group, after):
    rows, cols = queries[0].shape
    slots, heads, block_len, width = kv.shape
    offsets = len(queries)
    work = slots * heads * rows * block_len // GROUPS
    return pl.pallas_call(
        functools.partial(attend_kernel, group, offsets, len(after)),
        out_shape=[
            jax.ShapeDtypeStruct((offsets // 2, rows, cols), F32),
            jax.ShapeDtypeStruct((offsets // 2, rows, cols), BF16),
        ],
        in_specs=[SM] + [VM] * (1 + offsets) + [ANY] * len(after),
        out_specs=[VM, VM],
        scratch_shapes=[
            pltpu.VMEM((offsets, rows, cols), BF16),
            pltpu.VMEM((offsets, rows, cols), F32),
            pltpu.VMEM((2 * heads, rows, block_len // 2), BF16),
        ],
        compiler_params=params(),
        cost_estimate=pl.CostEstimate(
            flops=2 * work * width, bytes_accessed=2 * work // rows * width, transcendentals=work
        ),
        name=f"attend_{group}",
    )(plan, kv, *queries, *after)


def pair_kernel(near, far, *refs):
    outs = refs[-near.shape[0] :]
    for e, out in enumerate(outs):
        out[...] = (near[e] + far[e].astype(F32)).astype(out.dtype)


def pair_terms(near, far, dtype, after):
    chips, rows, cols = near.shape
    return pl.pallas_call(
        pair_kernel,
        out_shape=[jax.ShapeDtypeStruct((rows, cols), dtype)] * chips,
        in_specs=[VM, VM] + [ANY] * len(after),
        out_specs=[VM] * chips,
        compiler_params=params(),
        name="pair_terms",
    )(near, far, *after)


def add_kernel(*refs):
    acc = refs[0][...]
    for ref in refs[1:-1]:
        acc = acc + ref[...].astype(F32)
    refs[-1][...] = acc.astype(BF16)


def add_terms(terms):
    return pl.pallas_call(
        add_kernel,
        out_shape=jax.ShapeDtypeStruct(terms[0].shape, BF16),
        in_specs=[VM] * len(terms),
        out_specs=VM,
        compiler_params=params(),
        name="add_terms",
    )(*terms)


def finish_kernel(shape, cand_ref, gain_ref, weight_ref, *refs):
    parts = len(shape)
    out_ref, refs = refs[-1], list(refs[:-1])
    gate = [refs.pop(0) for _ in range(parts)]
    blocks = [sum(refs.pop(0)[...].astype(F32) for _ in range(n)) for n in shape]
    me = lax.axis_index("hist")
    cols = out_ref.shape[2]
    mean = sum(jnp.sum(b, axis=-1, keepdims=True) for b in blocks) / D
    blocks = [b - mean for b in blocks]
    var = sum(jnp.sum(b * b, axis=-1, keepdims=True) for b in blocks) / D
    rstd = lax.rsqrt(var + EPS)
    acc = cand_ref[0, :, pl.ds(pl.multiple_of(me * cols, DH), cols)].astype(F32)
    for k in range(parts):
        at = pl.ds(pl.multiple_of((me ^ k) * cols, DH), cols)
        gained = blocks[k] * rstd * gain_ref[:, at]
        gated = (gained * gate[k][...].astype(F32)).astype(BF16)
        acc = acc + jnp.dot(gated, weight_ref[at, :], preferred_element_type=F32)
    out_ref[0] = acc.astype(BF16)


def finish(candidates, attention_gain, out_weight, gate, attn):
    rows, cols = gate[0].shape
    flat = [x for group in attn for x in group]
    return pl.pallas_call(
        functools.partial(finish_kernel, [len(group) for group in attn]),
        out_shape=jax.ShapeDtypeStruct((1, rows, cols), BF16),
        in_specs=[VM] * (3 + len(gate) + len(flat)),
        out_specs=VM,
        compiler_params=params(),
        name="finish",
    )(candidates, attention_gain.reshape(1, D), out_weight, *gate, *flat)


def swap(x, axis, bit):
    n = lax.axis_size(axis)
    return lax.ppermute(x, axis, [(i, i ^ bit) for i in range(n)])


def exchange(x, axis):
    n = lax.axis_size(axis)
    if n != 4:
        return [[x]] + [[swap(x, axis, k)] for k in range(1, n)]
    one, two = swap(x, axis, 1), swap(x, axis, 2)
    mid = lax.ppermute(x, axis, [(1, 2), (2, 1)])
    ends = lax.ppermute(two, axis, [(2, 3), (1, 0)])
    return [[x], [one], [two], [mid, ends]]


def local(
    candidates,
    input_gain,
    proj_weight,
    history_cache,
    slot_user,
    slot_block,
    history_len,
    attention_gain,
    out_weight,
):
    parts = lax.axis_size("hist")
    chips = lax.axis_size("cand") // 2
    in_hbm = functools.partial(pltpu.with_memory_space_constraint, memory_space=pltpu.HBM)
    query_own, gate_own, plan = project(
        in_hbm(candidates),
        in_hbm(input_gain.reshape(1, D)),
        in_hbm(proj_weight),
        in_hbm(slot_user),
        in_hbm(slot_block),
        in_hbm(history_len),
        history_cache.shape[2],
        chips,
    )
    query_near = [query_own] + [swap(query_own, "cand", 2 * e) for e in range(1, chips)]
    query_far = [swap(q, "cand", 1) for q in query_near]
    gate = [gate_own] + [swap(gate_own, "hist", k) for k in range(1, parts)]
    kv = load(plan, in_hbm(history_cache))
    groups = groups_of(chips)
    last = len(groups) - 1
    near, far, sent = [], [], []

    def send(g, after):
        pairs = pair_terms(near[g], far[g], BF16, after)
        sent.append([swap(pair, "cand", 2 * e) for e, pair in zip(groups[g], pairs)])
        return pairs

    for g, group in enumerate(groups):
        queries = [q for e in group for q in (query_near[e], query_far[e])]
        after = near[-1:]
        if g == last:
            after += gate[1:]
            if g > 2:
                after += send(1, [])[:1]
        terms = attend(queries, kv, plan, g, after)
        near.append(terms[0])
        far.append(swap(terms[1], "cand", 1))
    for g in range(1 + len(sent), last + 1):
        send(g, sent[0][:1] if g == last and g > 1 else [])
    terms = list(pair_terms(near[0], far[0], F32, near[1:2]))
    terms += [t for group in sent for t in group]
    attn = exchange(add_terms(terms), "hist")
    return finish(candidates, attention_gain, out_weight, gate, attn)


def solution(mesh):
    return jax.shard_map(
        local,
        mesh=mesh,
        in_specs=(
            P("cand", None, None),
            P(),
            P(None, None, "hist"),
            P("cand", "hist", None, None),
            P("cand"),
            P("cand"),
            P(),
            P(),
            P(None, "hist"),
        ),
        out_specs=P("cand", None, "hist"),
        check_vma=False,
    )
```

```python
import functools

import jax
import jax.numpy as jnp
from jax import lax
from jax.experimental import pallas as pl
from jax.experimental.pallas import tpu as pltpu
from jax.sharding import PartitionSpec as P

D = 1024
DH = 128
EPS = 1e-05
GROUPS = 4
F32 = jnp.float32
BF16 = jnp.bfloat16
VMEM_BYTES = 12 * 1024 * 1024
CACHE_BYTES = 26 * 1024 * 1024
HALF_SCALE = 0.5 * DH ** (-0.5)

VM = pl.BlockSpec(memory_space=pltpu.VMEM)
SM = pl.BlockSpec(memory_space=pltpu.SMEM)
HB = pl.BlockSpec(memory_space=pltpu.HBM)
ANY = pl.BlockSpec(memory_space=pl.ANY)


def params(limit=VMEM_BYTES):
    return pltpu.CompilerParams(vmem_limit_bytes=limit)


def silu_of_half(half):
    return half * jnp.tanh(half) + half


SLOT, OFFSET, LIVE, COUNT = range(4)


def groups_of(chips):
    per = -(-(chips - 1) // (GROUPS - 1))
    return [[0]] + [list(range(at, min(at + per, chips))) for at in range(1, chips, per)]


def project_kernel(
    block_len, per, cand_hbm, gain_hbm, weight_hbm, user_hbm, block_hbm, len_hbm, *refs
):
    query_ref, gate_ref, plan, cand, gain, weight, user, block, length, sems, wsems = refs
    ints = [
        pltpu.make_async_copy(src, dst, sems.at[i])
        for i, (src, dst) in enumerate([(user_hbm, user), (block_hbm, block), (len_hbm, length)])
    ]
    rows_in = [
        pltpu.make_async_copy(src, dst, sems.at[3 + i])
        for i, (src, dst) in enumerate([(cand_hbm, cand), (gain_hbm, gain)])
    ]
    weights_in = [
        pltpu.make_async_copy(weight_hbm.at[i], weight.at[i], wsems.at[i]) for i in range(2)
    ]
    for copy in ints + rows_in + weights_in[::-1]:
        copy.start()
    me = lax.axis_index("cand")
    for copy in ints:
        copy.wait()
    for group in range(GROUPS):
        plan[group, COUNT, 0] = 0
    for s in range(user.shape[0]):
        owner, number = user[s], block[s]
        offset = owner ^ me
        group = (offset // 2 + per - 1) // per
        count = plan[group, COUNT, 0]
        live = jnp.where(number >= 0, length[owner] - number * block_len, 0)
        plan[group, SLOT, count] = s
        plan[group, OFFSET, count] = offset - jnp.where(group > 0, 2 * ((group - 1) * per + 1), 0)
        plan[GROUPS, LIVE, s] = live
        plan[group, COUNT, 0] = count + (number >= 0).astype(jnp.int32)

    for copy in rows_in:
        copy.wait()
    rows = cand[0].astype(F32)
    centred = rows - jnp.mean(rows, axis=-1, keepdims=True)
    var = jnp.mean(centred * centred, axis=-1, keepdims=True)
    normed = (centred * lax.rsqrt(var + EPS) * gain[...]).astype(BF16)
    weights_in[1].wait()
    half = 0.5 * jnp.dot(normed, weight[1], preferred_element_type=F32)
    query_ref[...] = (silu_of_half(half) * HALF_SCALE).astype(BF16)
    weights_in[0].wait()
    half = 0.5 * jnp.dot(normed, weight[0], preferred_element_type=F32)
    gate_ref[...] = silu_of_half(half).astype(BF16)


def project(
    candidates, input_gain, proj_weight, slot_user, slot_block, history_len, block_len, chips
):
    rows, cols = candidates.shape[1], proj_weight.shape[2]
    width = -(-(slot_user.shape[0] + 1) // 128) * 128
    per = -(-(chips - 1) // (GROUPS - 1))
    return pl.pallas_call(
        functools.partial(project_kernel, block_len, per),
        out_shape=[
            jax.ShapeDtypeStruct((rows, cols), BF16),
            jax.ShapeDtypeStruct((rows, cols), BF16),
            jax.ShapeDtypeStruct((GROUPS + 1, 4, width), jnp.int32),
        ],
        in_specs=[HB] * 6,
        out_specs=[VM, VM, SM],
        scratch_shapes=[
            pltpu.VMEM(candidates.shape, BF16),
            pltpu.VMEM((1, D), F32),
            pltpu.VMEM(proj_weight.shape, BF16),
            pltpu.SMEM(slot_user.shape, jnp.int32),
            pltpu.SMEM(slot_block.shape, jnp.int32),
            pltpu.SMEM(history_len.shape, jnp.int32),
            pltpu.SemaphoreType.DMA((5,)),
            pltpu.SemaphoreType.DMA((2,)),
        ],
        compiler_params=params(),
        cost_estimate=pl.CostEstimate(
            flops=4 * rows * cols * D, bytes_accessed=6 * cols * D, transcendentals=2 * rows * cols
        ),
        name="project",
    )(candidates, input_gain, proj_weight, slot_user, slot_block, history_len)


def load_kernel(plan, cache, kv, sems):
    slots, heads, block_len, _ = cache.shape

    def each_live(do):
        def visit(s, carry):
            @pl.when(plan[GROUPS, LIVE, s] > 0)
            def _():
                do(s)

            return carry

        lax.fori_loop(0, slots, visit, 0)

    def copy(s):
        return pltpu.make_async_copy(cache.at[s], kv.at[s], sems.at[s])

    def arrive(s):
        copy(s).wait()
        live = plan[GROUPS, LIVE, s]

        @pl.when(live < block_len)
        def _():
            event = lax.broadcasted_iota(jnp.int32, (block_len, DH), 0)
            for j in range(heads):
                vals = kv[s, j, :, DH:]
                kv[s, j, :, DH:] = jnp.where(event < live, vals, jnp.zeros_like(vals))

    each_live(lambda s: copy(s).start())
    each_live(arrive)


def load(plan, history_cache):
    return pl.pallas_call(
        load_kernel,
        out_shape=pltpu.VMEM(history_cache.shape, BF16),
        in_specs=[SM, HB],
        out_specs=VM,
        scratch_shapes=[pltpu.SemaphoreType.DMA((history_cache.shape[0],))],
        compiler_params=params(CACHE_BYTES),
        cost_estimate=pl.CostEstimate(
            flops=0, bytes_accessed=2 * history_cache.size, transcendentals=0
        ),
        name="load",
    )(plan, history_cache)


def attend_kernel(group, offsets, afters, plan, kv, *refs):
    queries, (near, far, query, total, wts) = refs[:offsets], refs[offsets + afters :]
    heads, block_len = kv.shape[1:3]
    half = block_len // 2
    tiles = [(j, e) for j in range(heads) for e in range(2)]
    count = plan[group, COUNT, 0]

    for d in range(offsets):
        query[d] = queries[d][...]
    total[...] = jnp.zeros_like(total)
    wts[...] = jnp.zeros_like(wts)

    def weigh(u, t):
        j, e = tiles[t]
        scores = lax.dot_general(
            query[plan[group, OFFSET, u], :, j * DH : (j + 1) * DH],
            kv[plan[group, SLOT, u], j, e * half : (e + 1) * half, :DH],
            (((1,), (1,)), ((), ())),
            preferred_element_type=F32,
        )
        wts[t] = silu_of_half(scores).astype(BF16)

    def gather(u, t):
        j, e = tiles[t]
        total[plan[group, OFFSET, u], :, j * DH : (j + 1) * DH] += jnp.dot(
            wts[t],
            kv[plan[group, SLOT, u], j, e * half : (e + 1) * half, DH:],
            preferred_element_type=F32,
        )

    last = len(tiles) - 1

    def step(u, carry):
        for t in range(len(tiles)):
            weigh(u, t)
            if t == 0:
                gather(jnp.maximum(u - 1, 0), last)
            else:
                gather(u, t - 1)
        return carry

    @pl.when(count > 0)
    def _():
        lax.fori_loop(0, count, step, 0)
        gather(count - 1, last)

    for d in range(offsets):
        if d % 2 == 0:
            near[d // 2] = total[d]
        else:
            far[d // 2] = total[d].astype(BF16)


def attend(queries, kv, plan, group, after):
    rows, cols = queries[0].shape
    slots, heads, block_len, width = kv.shape
    offsets = len(queries)
    work = slots * heads * rows * block_len // GROUPS
    return pl.pallas_call(
        functools.partial(attend_kernel, group, offsets, len(after)),
        out_shape=[
            jax.ShapeDtypeStruct((offsets // 2, rows, cols), F32),
            jax.ShapeDtypeStruct((offsets // 2, rows, cols), BF16),
        ],
        in_specs=[SM] + [VM] * (1 + offsets) + [ANY] * len(after),
        out_specs=[VM, VM],
        scratch_shapes=[
            pltpu.VMEM((offsets, rows, cols), BF16),
            pltpu.VMEM((offsets, rows, cols), F32),
            pltpu.VMEM((2 * heads, rows, block_len // 2), BF16),
        ],
        compiler_params=params(),
        cost_estimate=pl.CostEstimate(
            flops=2 * work * width, bytes_accessed=2 * work // rows * width, transcendentals=work
        ),
        name=f"attend_{group}",
    )(plan, kv, *queries, *after)


def pair_kernel(near, far, *refs):
    outs = refs[-near.shape[0] :]
    for e, out in enumerate(outs):
        out[...] = (near[e] + far[e].astype(F32)).astype(out.dtype)


def pair_terms(near, far, dtype, after):
    chips, rows, cols = near.shape
    return pl.pallas_call(
        pair_kernel,
        out_shape=[jax.ShapeDtypeStruct((rows, cols), dtype)] * chips,
        in_specs=[VM, VM] + [ANY] * len(after),
        out_specs=[VM] * chips,
        compiler_params=params(),
        name="pair_terms",
    )(near, far, *after)


def add_kernel(*refs):
    *terms, attn_ref, stats_ref = refs
    acc = terms[0][...]
    for ref in terms[1:]:
        acc = acc + ref[...].astype(F32)
    attn_ref[...] = acc
    total = jnp.sum(acc, axis=-1, keepdims=True)
    centred = acc - total / acc.shape[1]
    spread = jnp.sum(centred * centred, axis=-1, keepdims=True)
    lane = lax.broadcasted_iota(jnp.int32, (acc.shape[0], 128), 1)
    stats_ref[...] = jnp.where(lane == 0, total, spread).T[:8]


def add_terms(terms):
    rows, cols = terms[0].shape
    return pl.pallas_call(
        add_kernel,
        out_shape=[
            jax.ShapeDtypeStruct((rows, cols), F32),
            jax.ShapeDtypeStruct((8, rows), F32),
        ],
        in_specs=[VM] * len(terms),
        out_specs=[VM, VM],
        compiler_params=params(),
        name="add_terms",
    )(*terms)


def gate_kernel(attn_ref, gate_ref, gain_ref, *refs):
    *stats, out_ref = refs
    rows, cols = attn_ref.shape
    totals = [ref[0:1] for ref in stats]
    mean = sum(totals) / D
    var = sum(
        ref[1:2] + cols * (total / cols - mean) * (total / cols - mean)
        for ref, total in zip(stats, totals)
    )
    rstd = lax.rsqrt(var / D + EPS)
    line = lax.broadcasted_iota(jnp.int32, (128, rows), 0)
    both = jnp.where(line == 0, mean, rstd).T
    at = pl.ds(pl.multiple_of(lax.axis_index("hist") * cols, DH), cols)
    gained = (attn_ref[...] - both[:, 0:1]) * both[:, 1:2] * gain_ref[:, at]
    out_ref[...] = (gained * gate_ref[...].astype(F32)).astype(BF16)


def gate_rows(attn, gate, attention_gain, stats):
    return pl.pallas_call(
        gate_kernel,
        out_shape=jax.ShapeDtypeStruct(attn.shape, BF16),
        in_specs=[VM] * (3 + len(stats)),
        out_specs=VM,
        compiler_params=params(),
        name="gate_rows",
    )(attn, gate, attention_gain.reshape(1, D), *stats)


def finish_kernel(shape, cand_ref, weight_ref, *refs):
    out_ref, refs = refs[-1], list(refs[:-1])
    me = lax.axis_index("hist")
    cols = out_ref.shape[2]
    acc = cand_ref[0, :, pl.ds(pl.multiple_of(me * cols, DH), cols)].astype(F32)
    for k, n in enumerate(shape):
        at = pl.ds(pl.multiple_of((me ^ k) * cols, DH), cols)
        gated = sum(refs.pop(0)[...].astype(F32) for _ in range(n)).astype(BF16)
        acc = acc + jnp.dot(gated, weight_ref[at, :], preferred_element_type=F32)
    out_ref[0] = acc.astype(BF16)


def finish(candidates, out_weight, gated):
    rows, cols = gated[0][0].shape
    flat = [x for group in gated for x in group]
    return pl.pallas_call(
        functools.partial(finish_kernel, [len(group) for group in gated]),
        out_shape=jax.ShapeDtypeStruct((1, rows, cols), BF16),
        in_specs=[VM] * (2 + len(flat)),
        out_specs=VM,
        compiler_params=params(),
        name="finish",
    )(candidates, out_weight, *flat)


def swap(x, axis, bit):
    n = lax.axis_size(axis)
    return lax.ppermute(x, axis, [(i, i ^ bit) for i in range(n)])


def exchange(x, axis):
    n = lax.axis_size(axis)
    if n != 4:
        return [[x]] + [[swap(x, axis, k)] for k in range(1, n)]
    one, two = swap(x, axis, 1), swap(x, axis, 2)
    mid = lax.ppermute(x, axis, [(1, 2), (2, 1)])
    ends = lax.ppermute(two, axis, [(2, 3), (1, 0)])
    return [[x], [one], [two], [mid, ends]]


def local(
    candidates,
    input_gain,
    proj_weight,
    history_cache,
    slot_user,
    slot_block,
    history_len,
    attention_gain,
    out_weight,
):
    parts = lax.axis_size("hist")
    chips = lax.axis_size("cand") // 2
    in_hbm = functools.partial(pltpu.with_memory_space_constraint, memory_space=pltpu.HBM)
    query_own, gate_own, plan = project(
        in_hbm(candidates),
        in_hbm(input_gain.reshape(1, D)),
        in_hbm(proj_weight),
        in_hbm(slot_user),
        in_hbm(slot_block),
        in_hbm(history_len),
        history_cache.shape[2],
        chips,
    )
    query_near = [query_own] + [swap(query_own, "cand", 2 * e) for e in range(1, chips)]
    query_far = [swap(q, "cand", 1) for q in query_near]
    kv = load(plan, in_hbm(history_cache))
    groups = groups_of(chips)
    near, far, terms = {}, {}, []
    order = list(range(1, len(groups))) + [0]
    after = []
    for i, g in enumerate(order):
        queries = [q for e in groups[g] for q in (query_near[e], query_far[e])]
        near[g], ahead = attend(queries, kv, plan, g, after)
        far[g] = swap(ahead, "cand", 1)
        after = [near[g]]
        if i > 0:
            prev = order[i - 1]
            pairs = pair_terms(near[prev], far[prev], BF16, after)
            terms += [swap(pair, "cand", 2 * e) for e, pair in zip(groups[prev], pairs)]
            after = after + list(pairs[:1])
    terms = list(pair_terms(near[0], far[0], F32, [])) + terms
    attn, stats = add_terms(terms)
    stats = [stats] + [swap(stats, "hist", k) for k in range(1, parts)]
    gated = exchange(gate_rows(attn, gate_own, attention_gain, stats), "hist")
    return finish(candidates, out_weight, gated)


def solution(mesh):
    return jax.shard_map(
        local,
        mesh=mesh,
        in_specs=(
            P("cand", None, None),
            P(),
            P(None, None, "hist"),
            P("cand", "hist", None, None),
            P("cand"),
            P("cand"),
            P(),
            P(),
            P(None, "hist"),
        ),
        out_specs=P("cand", None, "hist"),
        check_vma=False,
    )
```

```python
import functools

import jax
import jax.numpy as jnp
from jax import lax
from jax.experimental import pallas as pl
from jax.experimental.pallas import tpu as pltpu
from jax.sharding import PartitionSpec as P

D = 1024
DH = 128
EPS = 1e-05
GROUPS = 3
F32 = jnp.float32
BF16 = jnp.bfloat16
VMEM_BYTES = 12 * 1024 * 1024
CACHE_BYTES = 26 * 1024 * 1024
HALF_SCALE = 0.5 * DH ** (-0.5)

VM = pl.BlockSpec(memory_space=pltpu.VMEM)
SM = pl.BlockSpec(memory_space=pltpu.SMEM)
HB = pl.BlockSpec(memory_space=pltpu.HBM)
ANY = pl.BlockSpec(memory_space=pl.ANY)


def params(limit=VMEM_BYTES):
    return pltpu.CompilerParams(vmem_limit_bytes=limit)


def silu_of_half(half):
    return half * jnp.tanh(half) + half


SLOT, OFFSET, LIVE, COUNT = range(4)


def groups_of(chips):
    per = -(-(chips - 1) // (GROUPS - 1))
    return [[0]] + [list(range(at, min(at + per, chips))) for at in range(1, chips, per)]


def project_kernel(
    block_len, per, cand_hbm, gain_hbm, weight_hbm, user_hbm, block_hbm, len_hbm, *refs
):
    query_ref, gate_ref, plan, cand, gain, weight, user, block, length, sems, wsems = refs
    ints = [
        pltpu.make_async_copy(src, dst, sems.at[i])
        for i, (src, dst) in enumerate([(user_hbm, user), (block_hbm, block), (len_hbm, length)])
    ]
    rows_in = [
        pltpu.make_async_copy(src, dst, sems.at[3 + i])
        for i, (src, dst) in enumerate([(cand_hbm, cand), (gain_hbm, gain)])
    ]
    weights_in = [
        pltpu.make_async_copy(weight_hbm.at[i], weight.at[i], wsems.at[i]) for i in range(2)
    ]
    for copy in ints + rows_in + weights_in[::-1]:
        copy.start()
    me = lax.axis_index("cand")
    for copy in ints:
        copy.wait()
    for group in range(GROUPS):
        plan[group, COUNT, 0] = 0
    for s in range(user.shape[0]):
        owner, number = user[s], block[s]
        offset = owner ^ me
        group = (offset // 2 + per - 1) // per
        count = plan[group, COUNT, 0]
        live = jnp.where(number >= 0, length[owner] - number * block_len, 0)
        plan[group, SLOT, count] = s
        plan[group, OFFSET, count] = offset - jnp.where(group > 0, 2 * ((group - 1) * per + 1), 0)
        plan[GROUPS, LIVE, s] = live
        plan[group, COUNT, 0] = count + (number >= 0).astype(jnp.int32)

    for copy in rows_in:
        copy.wait()
    rows = cand[0].astype(F32)
    centred = rows - jnp.mean(rows, axis=-1, keepdims=True)
    var = jnp.mean(centred * centred, axis=-1, keepdims=True)
    normed = (centred * lax.rsqrt(var + EPS) * gain[...]).astype(BF16)
    weights_in[1].wait()
    half = 0.5 * jnp.dot(normed, weight[1], preferred_element_type=F32)
    query_ref[...] = (silu_of_half(half) * HALF_SCALE).astype(BF16)
    weights_in[0].wait()
    half = 0.5 * jnp.dot(normed, weight[0], preferred_element_type=F32)
    gate_ref[...] = silu_of_half(half).astype(BF16)


def project(
    candidates, input_gain, proj_weight, slot_user, slot_block, history_len, block_len, chips
):
    rows, cols = candidates.shape[1], proj_weight.shape[2]
    width = -(-(slot_user.shape[0] + 1) // 128) * 128
    per = -(-(chips - 1) // (GROUPS - 1))
    return pl.pallas_call(
        functools.partial(project_kernel, block_len, per),
        out_shape=[
            jax.ShapeDtypeStruct((rows, cols), BF16),
            jax.ShapeDtypeStruct((rows, cols), BF16),
            jax.ShapeDtypeStruct((GROUPS + 1, 4, width), jnp.int32),
        ],
        in_specs=[HB] * 6,
        out_specs=[VM, VM, SM],
        scratch_shapes=[
            pltpu.VMEM(candidates.shape, BF16),
            pltpu.VMEM((1, D), F32),
            pltpu.VMEM(proj_weight.shape, BF16),
            pltpu.SMEM(slot_user.shape, jnp.int32),
            pltpu.SMEM(slot_block.shape, jnp.int32),
            pltpu.SMEM(history_len.shape, jnp.int32),
            pltpu.SemaphoreType.DMA((5,)),
            pltpu.SemaphoreType.DMA((2,)),
        ],
        compiler_params=params(),
        cost_estimate=pl.CostEstimate(
            flops=4 * rows * cols * D, bytes_accessed=6 * cols * D, transcendentals=2 * rows * cols
        ),
        name="project",
    )(candidates, input_gain, proj_weight, slot_user, slot_block, history_len)


def load_kernel(plan, cache, kv, sems):
    slots, heads, block_len, _ = cache.shape

    def each_live(do):
        def visit(s, carry):
            @pl.when(plan[GROUPS, LIVE, s] > 0)
            def _():
                do(s)

            return carry

        lax.fori_loop(0, slots, visit, 0)

    def copy(s):
        return pltpu.make_async_copy(cache.at[s], kv.at[s], sems.at[s])

    def arrive(s):
        copy(s).wait()
        live = plan[GROUPS, LIVE, s]

        @pl.when(live < block_len)
        def _():
            event = lax.broadcasted_iota(jnp.int32, (block_len, DH), 0)
            for j in range(heads):
                vals = kv[s, j, :, DH:]
                kv[s, j, :, DH:] = jnp.where(event < live, vals, jnp.zeros_like(vals))

    each_live(lambda s: copy(s).start())
    each_live(arrive)


def load(plan, history_cache):
    return pl.pallas_call(
        load_kernel,
        out_shape=pltpu.VMEM(history_cache.shape, BF16),
        in_specs=[SM, HB],
        out_specs=VM,
        scratch_shapes=[pltpu.SemaphoreType.DMA((history_cache.shape[0],))],
        compiler_params=params(CACHE_BYTES),
        cost_estimate=pl.CostEstimate(
            flops=0, bytes_accessed=2 * history_cache.size, transcendentals=0
        ),
        name="load",
    )(plan, history_cache)


def follow(x, first):
    return pl.pallas_call(
        lambda x_ref, first_ref, out_ref: None,
        out_shape=jax.ShapeDtypeStruct(x.shape, x.dtype),
        in_specs=[ANY, ANY],
        out_specs=ANY,
        input_output_aliases={0: 0},
        compiler_params=params(),
        name="follow",
    )(x, first)


def attend_kernel(group, offsets, afters, plan, kv, *refs):
    queries, (near, far, query, total, wts) = refs[:offsets], refs[offsets + afters :]
    heads, block_len = kv.shape[1:3]
    half = block_len // 2
    tiles = [(j, e) for j in range(heads) for e in range(2)]
    count = plan[group, COUNT, 0]

    for d in range(offsets):
        query[d] = queries[d][...]
    total[...] = jnp.zeros_like(total)
    wts[...] = jnp.zeros_like(wts)

    def weigh(u, t):
        j, e = tiles[t]
        scores = lax.dot_general(
            query[plan[group, OFFSET, u], :, j * DH : (j + 1) * DH],
            kv[plan[group, SLOT, u], j, e * half : (e + 1) * half, :DH],
            (((1,), (1,)), ((), ())),
            preferred_element_type=F32,
        )
        wts[t] = silu_of_half(scores).astype(BF16)

    def gather(u, t):
        j, e = tiles[t]
        total[plan[group, OFFSET, u], :, j * DH : (j + 1) * DH] += jnp.dot(
            wts[t],
            kv[plan[group, SLOT, u], j, e * half : (e + 1) * half, DH:],
            preferred_element_type=F32,
        )

    last = len(tiles) - 1

    def step(u, carry):
        for t in range(len(tiles)):
            weigh(u, t)
            if t == 0:
                gather(jnp.maximum(u - 1, 0), last)
            else:
                gather(u, t - 1)
        return carry

    @pl.when(count > 0)
    def _():
        lax.fori_loop(0, count, step, 0)
        gather(count - 1, last)

    for d in range(offsets):
        if d % 2 == 0:
            near[d // 2] = total[d]
        else:
            far[d // 2] = total[d].astype(BF16)


def attend(queries, kv, plan, group, after):
    rows, cols = queries[0].shape
    slots, heads, block_len, width = kv.shape
    offsets = len(queries)
    work = slots * heads * rows * block_len // GROUPS
    return pl.pallas_call(
        functools.partial(attend_kernel, group, offsets, len(after)),
        out_shape=[
            jax.ShapeDtypeStruct((offsets // 2, rows, cols), F32),
            jax.ShapeDtypeStruct((offsets // 2, rows, cols), BF16),
        ],
        in_specs=[SM] + [VM] * (1 + offsets) + [ANY] * len(after),
        out_specs=[VM, VM],
        scratch_shapes=[
            pltpu.VMEM((offsets, rows, cols), BF16),
            pltpu.VMEM((offsets, rows, cols), F32),
            pltpu.VMEM((2 * heads, rows, block_len // 2), BF16),
        ],
        compiler_params=params(),
        cost_estimate=pl.CostEstimate(
            flops=2 * work * width, bytes_accessed=2 * work // rows * width, transcendentals=work
        ),
        name=f"attend_{group}",
    )(plan, kv, *queries, *after)


def pair_kernel(near, far, *refs):
    outs = refs[-near.shape[0] :]
    for e, out in enumerate(outs):
        out[...] = (near[e] + far[e].astype(F32)).astype(out.dtype)


def pair_terms(near, far, dtype, after):
    chips, rows, cols = near.shape
    return pl.pallas_call(
        pair_kernel,
        out_shape=[jax.ShapeDtypeStruct((rows, cols), dtype)] * chips,
        in_specs=[VM, VM] + [ANY] * len(after),
        out_specs=[VM] * chips,
        compiler_params=params(),
        name="pair_terms",
    )(near, far, *after)


def add_kernel(*refs):
    *terms, attn_ref, stats_ref = refs
    acc = terms[0][...]
    for ref in terms[1:]:
        acc = acc + ref[...].astype(F32)
    attn_ref[...] = acc
    total = jnp.sum(acc, axis=-1, keepdims=True)
    centred = acc - total / acc.shape[1]
    spread = jnp.sum(centred * centred, axis=-1, keepdims=True)
    lane = lax.broadcasted_iota(jnp.int32, (acc.shape[0], 128), 1)
    stats_ref[...] = jnp.where(lane == 0, total, spread).T[:8]


def add_terms(terms):
    rows, cols = terms[0].shape
    return pl.pallas_call(
        add_kernel,
        out_shape=[
            jax.ShapeDtypeStruct((rows, cols), F32),
            jax.ShapeDtypeStruct((8, rows), F32),
        ],
        in_specs=[VM] * len(terms),
        out_specs=[VM, VM],
        compiler_params=params(),
        name="add_terms",
    )(*terms)


def gate_kernel(attn_ref, gate_ref, gain_ref, *refs):
    *stats, out_ref = refs
    rows, cols = attn_ref.shape
    totals = [ref[0:1] for ref in stats]
    mean = sum(totals) / D
    var = sum(
        ref[1:2] + cols * (total / cols - mean) * (total / cols - mean)
        for ref, total in zip(stats, totals)
    )
    rstd = lax.rsqrt(var / D + EPS)
    line = lax.broadcasted_iota(jnp.int32, (128, rows), 0)
    both = jnp.where(line == 0, mean, rstd).T
    at = pl.ds(pl.multiple_of(lax.axis_index("hist") * cols, DH), cols)
    gained = (attn_ref[...] - both[:, 0:1]) * both[:, 1:2] * gain_ref[:, at]
    out_ref[...] = (gained * gate_ref[...].astype(F32)).astype(BF16)


def gate_rows(attn, gate, attention_gain, stats):
    return pl.pallas_call(
        gate_kernel,
        out_shape=jax.ShapeDtypeStruct(attn.shape, BF16),
        in_specs=[VM] * (3 + len(stats)),
        out_specs=VM,
        compiler_params=params(),
        name="gate_rows",
    )(attn, gate, attention_gain.reshape(1, D), *stats)


def finish_kernel(shape, cand_ref, weight_ref, *refs):
    out_ref, refs = refs[-1], list(refs[:-1])
    me = lax.axis_index("hist")
    cols = out_ref.shape[2]
    acc = cand_ref[0, :, pl.ds(pl.multiple_of(me * cols, DH), cols)].astype(F32)
    for k, n in enumerate(shape):
        at = pl.ds(pl.multiple_of((me ^ k) * cols, DH), cols)
        gated = sum(refs.pop(0)[...].astype(F32) for _ in range(n)).astype(BF16)
        acc = acc + jnp.dot(gated, weight_ref[at, :], preferred_element_type=F32)
    out_ref[0] = acc.astype(BF16)


def finish(candidates, out_weight, gated):
    rows, cols = gated[0][0].shape
    flat = [x for group in gated for x in group]
    return pl.pallas_call(
        functools.partial(finish_kernel, [len(group) for group in gated]),
        out_shape=jax.ShapeDtypeStruct((1, rows, cols), BF16),
        in_specs=[VM] * (2 + len(flat)),
        out_specs=VM,
        compiler_params=params(),
        name="finish",
    )(candidates, out_weight, *flat)


def swap(x, axis, bit):
    n = lax.axis_size(axis)
    return lax.ppermute(x, axis, [(i, i ^ bit) for i in range(n)])


def exchange(x, axis):
    n = lax.axis_size(axis)
    if n != 4:
        return [[x]] + [[swap(x, axis, k)] for k in range(1, n)]
    one, two = swap(x, axis, 1), swap(x, axis, 2)
    mid = lax.ppermute(x, axis, [(1, 2), (2, 1)])
    ends = lax.ppermute(two, axis, [(2, 3), (1, 0)])
    return [[x], [one], [two], [mid, ends]]


def local(
    candidates,
    input_gain,
    proj_weight,
    history_cache,
    slot_user,
    slot_block,
    history_len,
    attention_gain,
    out_weight,
):
    parts = lax.axis_size("hist")
    chips = lax.axis_size("cand") // 2
    in_hbm = functools.partial(pltpu.with_memory_space_constraint, memory_space=pltpu.HBM)
    query_own, gate_own, plan = project(
        in_hbm(candidates),
        in_hbm(input_gain.reshape(1, D)),
        in_hbm(proj_weight),
        in_hbm(slot_user),
        in_hbm(slot_block),
        in_hbm(history_len),
        history_cache.shape[2],
        chips,
    )
    query_near = [query_own] + [swap(query_own, "cand", 2 * e) for e in range(1, chips)]
    kv = load(plan, in_hbm(history_cache))
    query_near = [query_own] + [follow(q, kv) for q in query_near[1:]]
    query_far = [swap(q, "cand", 1) for q in query_near]
    groups = groups_of(chips)
    near, far, terms = {}, {}, []
    order = list(range(1, len(groups))) + [0]
    after = []
    for i, g in enumerate(order):
        queries = [q for e in groups[g] for q in (query_near[e], query_far[e])]
        near[g], ahead = attend(queries, kv, plan, g, after)
        far[g] = swap(ahead, "cand", 1)
        after = [near[g]]
        if i > 0:
            prev = order[i - 1]
            pairs = pair_terms(near[prev], far[prev], BF16, after + terms[:1])
            terms += [swap(pair, "cand", 2 * e) for e, pair in zip(groups[prev], pairs)]
            after = after + list(pairs[:1])
    terms = list(pair_terms(near[0], far[0], F32, [])) + terms
    attn, stats = add_terms(terms)
    stats = [stats] + [swap(stats, "hist", k) for k in range(1, parts)]
    gated = exchange(gate_rows(attn, gate_own, attention_gain, stats), "hist")
    return finish(candidates, out_weight, gated)


def solution(mesh):
    return jax.shard_map(
        local,
        mesh=mesh,
        in_specs=(
            P("cand", None, None),
            P(),
            P(None, None, "hist"),
            P("cand", "hist", None, None),
            P("cand"),
            P("cand"),
            P(),
            P(),
            P(None, "hist"),
        ),
        out_specs=P("cand", None, "hist"),
        check_vma=False,
    )
```
